512 devices in a mesh: dom: 32 (over x, z_hi, core), cuts: 16 (over z_lo, y).
Axes of the slice: x: 4, y: 4, z: 16 (z_hi: 4, z_lo: 4; z = z_hi * 4 + z_lo), core: 2. Of those that a mesh axis runs over, the one named last changes fastest.
Arguments:
- src_table: float32 [131072, 256], P(('dom', 'cuts')), may hold values from -3 to 3
- src_state: float32 [131072], P(('dom', 'cuts')), may hold values from 0.0001 to 0.1
- dst_table: float32 [131072, 256], P(('dom', 'cuts')), may hold values from 0 to 1.2
- dst_state: float32 [131072], P(('dom', 'cuts')), may hold values from 0.0001 to 0.1
- relations: float32 [400, 256], replicated, may hold values from -3 to 3
- rel_state: float32 [400], replicated, may hold values from 0.0001 to 0.1
- src_rows: int32 [2, 262144], P(None, ('dom', 'cuts')), may hold values from 0 to 255
- dst_rows: int32 [2, 262144], P(None, ('dom', 'cuts')), may hold values from 0 to 255
- rel_ids: int32 [2, 262144], P(None, ('dom', 'cuts')), may hold values from 0 to 399
- neg_rows: int32 [2, 32768], P(None, ('dom', 'cuts')), may hold values from 0 to 255
Outputs:
- src_out: float32 [131072, 256], P(('dom', 'cuts'))
- src_state_out: float32 [131072], P(('dom', 'cuts'))
- dst_out: float32 [131072, 256], P(('dom', 'cuts'))
- dst_state_out: float32 [131072], P(('dom', 'cuts'))
- rel_out: float32 [400, 256], replicated
- rel_state_out: float32 [400], replicated
The draws below stay inside these ranges and needn't reach their ends.
All inputs are finite; a program needn't handle non-finite values.
Results may differ from the reference program's by a relative error of at most 0.0003.
The reference program's roundings to bfloat16 on the way (of `gb`) count: a program that leaves them out, or rounds other values in their place, can miss the bound.
Values may be sent and summed in bfloat16 or wider, within the bound.
A program may use at most 64 MiB of HBM per device.

```python
import math
import jax
import jax.numpy as jnp
import numpy as np
from jax import lax

D = 256
REL = 400
ROWS = 256
EDGES = 512
NEG_DEV = 64
NEG = 1024
ENT = 131072
N_DOM = 32
N_CUTS = 16


def with_ends(drawn, key, low, top_value):
    index_at = [jax.random.randint(jax.random.fold_in(key, axis), (), 0, length) for axis, length in enumerate(drawn.shape)]
    widest = drawn.shape.index(max(drawn.shape))
    next_to = index_at[:widest] + [(index_at[widest] + 1) % drawn.shape[widest]] + index_at[widest + 1:]
    return drawn.at[tuple(index_at)].set(low).at[tuple(next_to)].set(top_value)


def levels(stream_key, dims, pieces, low, top_value):
    level, own = 1.0, jax.random.fold_in(stream_key, 6)
    for dim, shards_of in pieces:
        steps = jnp.exp(jax.random.uniform(jax.random.fold_in(own, dim), (shards_of,), jnp.float32, low / len(pieces), top_value / len(pieces)))
        level = level * jnp.repeat(steps, dims[dim] // shards_of).reshape([-1 if axis == dim else 1 for axis in range(len(dims))])
    return level


def cumulative_ranks(amount, lean):
    loads = [(1 << 20) // math.isqrt(standing ** lean) + 1 for standing in range(1, amount + 1)]
    deviation = 1 + sum(loads) // (1 << 30)
    return np.cumsum(np.array([max(1, weight // deviation) for weight in loads]))


def skewed_ids(rng, shape, number_of, skew):
    listing = cumulative_ranks(number_of, skew)
    ticket = jax.random.randint(jax.random.fold_in(rng, 1), shape, 0, int(listing[number_of - 1]))
    standing = jnp.searchsorted(jnp.asarray(listing, jnp.int32), ticket, side="right")
    return jax.random.permutation(jax.random.fold_in(rng, 2), number_of)[standing].astype(jnp.int32)


def centred(rng, dims, scale, bound, shards=(), dtype=jnp.bfloat16):
    loudness = levels(rng, dims, shards, -0.22, 0.18) if shards else 1.0
    array = jax.random.normal(rng, dims, jnp.float32) * scale * loudness
    return jnp.minimum(jnp.maximum(array, -bound), bound).astype(dtype)


def setup_inputs(seed: int = 0) -> dict:
    key_list = jax.random.split(jax.random.key(seed), 11)
    return {
        "src_table": centred(key_list[0], (ENT, D), 0.6, 3.0, ((0, 512),), jnp.float32),
        "src_state": jnp.clip(jnp.exp(math.log(0.1) - 6.9077553 * jax.random.uniform(key_list[1], (ENT,), jnp.float32) ** levels(key_list[1], (ENT,), ((0, 512),), -0.2, 0.2)), 0.0001, 0.1),
        "dst_table": jnp.clip(1.2 * jax.random.uniform(key_list[2], (ENT, D), jnp.float32) ** levels(key_list[2], (ENT, D), ((0, 512),), -0.2, 0.2), 0.0, 1.2),
        "dst_state": jnp.clip(jnp.exp(math.log(0.1) - 6.9077553 * jax.random.uniform(key_list[3], (ENT,), jnp.float32) ** levels(key_list[3], (ENT,), ((0, 512),), -0.2, 0.2)), 0.0001, 0.1),
        "relations": centred(key_list[4], (REL, D), 0.6, 3.0, (), jnp.float32),
        "rel_state": jnp.clip(jnp.exp(jax.random.uniform(key_list[5], (REL,), jnp.float32, math.log(0.0001), math.log(0.1))), 0.0001, 0.1),
        "src_rows": with_ends(jax.random.randint(key_list[6], (2, EDGES * N_DOM * N_CUTS), 0, ROWS), jax.random.fold_in(key_list[6], 1), 0, ROWS - 1).astype(jnp.int32),
        "dst_rows": with_ends(jax.random.randint(key_list[7], (2, EDGES * N_DOM * N_CUTS), 0, ROWS), jax.random.fold_in(key_list[7], 1), 0, ROWS - 1).astype(jnp.int32),
        "rel_ids": with_ends(skewed_ids(key_list[8], (2, EDGES * N_DOM * N_CUTS), REL, 2), jax.random.fold_in(key_list[8], 3), 0, REL - 1).astype(jnp.int32),
        "neg_rows": with_ends(jax.random.randint(key_list[9], (2, NEG_DEV * N_DOM * N_CUTS), 0, ROWS), jax.random.fold_in(key_list[9], 1), 0, ROWS - 1).astype(jnp.int32),
    }


learn_rate = 0.1

def complex_mul(left, right):
    half = left.shape[-1] // 2
    lr, li = (left[..., :half], left[..., half:])
    rr, ri = (right[..., :half], right[..., half:])
    return jnp.concatenate([lr * rr - li * ri, lr * ri + li * rr], axis=-1)

def complex_back(grad_q, other):
    half = grad_q.shape[-1] // 2
    gr, gi = (grad_q[..., :half], grad_q[..., half:])
    orr, oi = (other[..., :half], other[..., half:])
    return jnp.concatenate([gr * orr + gi * oi, -gr * oi + gi * orr], axis=-1)

def adagrad(weights, state, grad):
    state_new = state + lax.optimization_barrier(jnp.mean(grad * grad, axis=-1))
    return (weights - learn_rate * grad / jnp.sqrt(state_new)[..., None], state_new)

def pick_rows(table, index):
    return jax.vmap(lambda tab, idx: tab[idx])(table, index)

def add_rows(grad, index, rows):
    return jax.vmap(lambda idx, val: jnp.zeros((ROWS, D), jnp.float32).at[idx].add(val))(index, rows)

def reference(src_table, src_state, dst_table, dst_state, relations, rel_state, src_rows, dst_rows, rel_ids, neg_rows):
    source = src_table.reshape(N_DOM, N_CUTS, ROWS, D)
    source_st = src_state.reshape(N_DOM, N_CUTS, ROWS)
    target = dst_table.reshape(N_DOM, N_CUTS, ROWS, D)
    target_st = dst_state.reshape(N_DOM, N_CUTS, ROWS)
    rel, rel_st = (relations, rel_state)
    src_idx = src_rows.reshape(2, N_DOM, N_CUTS, EDGES)
    dst_idx = dst_rows.reshape(2, N_DOM, N_CUTS, EDGES)
    rel_idx = rel_ids.reshape(2, N_DOM, N_CUTS, EDGES)
    neg_idx = neg_rows.reshape(2, N_DOM, N_CUTS, NEG_DEV)
    for rnd in range(2):

        def group(items):
            src_g, dst_g, sidx, didx, ridx, nidx = items
            svec = pick_rows(src_g, sidx).reshape(-1, D)
            tvec = pick_rows(dst_g, didx).reshape(-1, D)
            rvec = rel[ridx.reshape(-1)]
            negs = pick_rows(dst_g, nidx).reshape(-1, D).astype(jnp.bfloat16)
            qvec = complex_mul(svec, rvec)
            pos = lax.optimization_barrier(jnp.sum(qvec * tvec, axis=-1))
            qb = qvec.astype(jnp.bfloat16)
            scores = jnp.dot(qb, negs.T, preferred_element_type=jnp.float32)
            gb = (jax.nn.sigmoid(scores) / NEG).astype(jnp.bfloat16)
            coef = -jax.nn.sigmoid(-pos)
            grad_q = coef[:, None] * tvec + jnp.dot(gb, negs, preferred_element_type=jnp.float32)
            grad_t = coef[:, None] * qvec
            grad_neg = jnp.dot(gb.T, qb, preferred_element_type=jnp.float32).reshape(N_CUTS, NEG_DEV, D)
            grad_s = complex_back(grad_q, rvec)
            grad_r = complex_back(grad_q, svec)
            gsrc = add_rows(None, sidx, grad_s.reshape(N_CUTS, EDGES, D))
            gdst = add_rows(None, didx, grad_t.reshape(N_CUTS, EDGES, D)) + add_rows(None, nidx, grad_neg)
            grel = jnp.zeros((REL, D), jnp.float32).at[ridx.reshape(-1)].add(grad_r)
            return (gsrc, gdst, grel)
        gsrc, gdst, grel = lax.map(group, (source, target, src_idx[rnd], dst_idx[rnd], rel_idx[rnd], neg_idx[rnd]))
        source, source_st = adagrad(source, source_st, gsrc)
        target, target_st = adagrad(target, target_st, gdst)
        rel, rel_st = adagrad(rel, rel_st, lax.optimization_barrier(jnp.sum(grel, axis=0)))
        if rnd == 0:
            target = jnp.roll(target, N_DOM // 2, axis=0)
            target_st = jnp.roll(target_st, N_DOM // 2, axis=0)
    return (source.reshape(ENT, D), source_st.reshape(ENT), target.reshape(ENT, D), target_st.reshape(ENT), rel, rel_st)
```

```python
import functools

import jax
import jax.numpy as jnp
from jax import lax
from jax.experimental import pallas as pl
from jax.experimental.pallas import tpu as pltpu
from jax.sharding import PartitionSpec as P

RATE = 0.1
MESH = pl.DeviceIdType.MESH
f32, bf16, i32 = jnp.float32, jnp.bfloat16, jnp.int32

AG_Z, AG_Y, AG_F = 0, 3, 6
RS_Y, RS_Z = 15, 27
MOVE, PAIR_A, ZL_A, ZH, ZL_B, PAIR_B = 30, 32, 33, 36, 39, 42
XY_A, XY_B = 43, 59
SEMS = 75


def split2(x):
    hi = x.astype(bf16)
    return hi, (x - hi.astype(f32)).astype(bf16)


def columns(row):
    return jnp.broadcast_to(row, (128, row.shape[1])).T


def pick(col_idx, width):
    lane = lax.broadcasted_iota(i32, col_idx.shape, 1)
    parts = [jnp.where(col_idx == lane + 128 * j, 1.0, 0.0) for j in range(width // 128)]
    return jnp.concatenate(parts, axis=1).astype(bf16)


def spread(row_idx, width):
    at = lax.broadcasted_iota(i32, (width, row_idx.shape[1]), 0)
    return jnp.where(at == row_idx, 1.0, 0.0).astype(bf16)


def exact_dot(ones, x):
    wide = x.shape[1]
    out = jnp.dot(ones, jnp.concatenate(split2(x), axis=1), preferred_element_type=f32)
    return out[:, :wide] + out[:, wide:]


def back(grad, other):
    h = grad.shape[1] // 2
    gr, gi, orr, oi = grad[:, :h], grad[:, h:], other[:, :h], other[:, h:]
    return jnp.concatenate([gr * orr + gi * oi, gi * orr - gr * oi], axis=1)


def adagrad(w, state, g):
    state = state + jnp.sum(g * g, axis=1, keepdims=True) * (1.0 / g.shape[1])
    scale = RATE / jnp.sqrt(state)
    return w - g * jnp.concatenate([scale] * (g.shape[1] // 128), axis=1), state


def kernel(
    s_in, ss_in, t_in, ts_in, r_in, rs_in, sidx, didx, ridx, nidx,
    s_out, ss_out, t_out, ts_out, r_out, rs_out,
    negs, dn_f, dn_b, rs_y, z_b, rs_z, t_new, ts_new, t_got, ts_got,
    gr, pair, part, xy, piece, zl, tile, zh, done,
    s_tab, s_st, t_st, r_tab, r_st, q_v, t_v, r_v, s_v, dq,
    ssem, rsem,
):
    dom, cuts = lax.axis_index("dom"), lax.axis_index("cuts")
    x, z_hi, core = dom // 8, (dom // 2) % 4, dom % 2
    z_lo, y = cuts // 4, cuts % 4
    spot = x * 4 + y
    rels = r_in.shape[0]
    waits = []

    def device(x_=None, z_hi_=None, core_=None, z_lo_=None, y_=None):
        a = x if x_ is None else x_
        b = z_hi if z_hi_ is None else z_hi_
        c = core if core_ is None else core_
        d = z_lo if z_lo_ is None else z_lo_
        e = y if y_ is None else y_
        return (a * 8 + b * 2 + c, d * 4 + e)

    def hop(v, o):
        return (v + o) % 4

    def at_spot(o):
        p = (spot + o) % 16
        return p, device(x_=p // 4, y_=p % 4)

    def remote(k, n, src, dst, dev):
        return pltpu.make_async_remote_copy(
            src_ref=src, dst_ref=dst, send_sem=ssem.at[k, n], recv_sem=rsem.at[k, n],
            device_id=dev, device_id_type=MESH,
        )

    def send(*args):
        copy = remote(*args)
        copy.start()
        waits.append(copy)
        return copy

    other = device(core_=1 - core)
    across = device(x_=hop(x, 2))

    barrier = pltpu.get_barrier_semaphore()

    def greet(o, _):
        pl.semaphore_signal(barrier, inc=1, device_id=at_spot(o)[1], device_id_type=MESH)
        return 0

    lax.fori_loop(1, 16, greet, 0)
    for o in (1, 2, 3):
        pl.semaphore_signal(barrier, inc=1, device_id=device(z_lo_=hop(z_lo, o)), device_id_type=MESH)
        pl.semaphore_signal(barrier, inc=1, device_id=device(z_hi_=hop(z_hi, o)), device_id_type=MESH)
    pl.semaphore_signal(barrier, inc=1, device_id=other, device_id_type=MESH)

    ncol = columns(nidx[...])
    half = nidx.shape[1] // 2
    n_rows = nidx.shape[1] // 2

    def my_negs(k, table):
        ones = pick(ncol[k * half : (k + 1) * half], table.shape[0])
        negs[k, z_lo, y] = jnp.dot(ones, table.astype(bf16), preferred_element_type=f32).astype(bf16)

    def send_negs(k):
        own = negs.at[k, z_lo, y]
        for o in (1, 2, 3):
            send(k, AG_Z + o - 1, own, own, device(z_lo_=hop(z_lo, o)))
        for o in (1, 2, 3):
            send(k, AG_Y + o - 1, own, own, device(y_=hop(y, o)))

    def forward_negs(k):
        for o in (1, 2, 3):
            block = negs.at[k, hop(z_lo, 4 - o), y]
            remote(k, AG_Z + o - 1, block, block, across).wait_recv()
            for p in (1, 2, 3):
                send(k, AG_F + 3 * (o - 1) + p - 1, block, block, device(y_=hop(y, p)))

    def wait_group(k, o):
        first = AG_Y if o == 0 else AG_F + 3 * (o - 1)
        for p in (1, 2, 3):
            block = negs.at[k, hop(z_lo, 4 - o), hop(y, 4 - p)]
            remote(k, first + p - 1, block, block, across).wait_recv()

    def gather_st(k, table):
        s_v[...] = exact_dot(pick(columns(sidx[k : k + 1, :]), 256), s_tab[...])
        t_v[...] = exact_dot(pick(columns(didx[k : k + 1, :]), 256), table)

    def gather_r(k):
        r_v[...] = exact_dot(pick(columns(ridx[k : k + 1, :]), 512), r_tab[...])

    def edges(k):
        s, r = s_v[...], r_v[...]
        h = s.shape[1] // 2
        sr, si, rr, ri = s[:, :h], s[:, h:], r[:, :h], r[:, h:]
        q = jnp.concatenate([sr * rr - si * ri, sr * ri + si * rr], axis=1)
        q_v[...] = q.astype(bf16)
        t = t_v[...]
        coef = -jax.nn.sigmoid(-jnp.sum(q * t, axis=1, keepdims=True))
        dq[...] = coef * t
        return exact_dot(spread(didx[k : k + 1, :], 256), coef * q)

    def group(k, o):
        at = hop(z_lo, 4 - o)
        block = negs[k, at].reshape(4 * n_rows, 256)
        qb = q_v[...]
        scores = lax.dot_general(qb, block, (((1,), (1,)), ((), ())), preferred_element_type=f32)
        gb = (jax.nn.sigmoid(scores) * (1.0 / (16 * n_rows))).astype(bf16)
        dq[...] += jnp.dot(gb, block, preferred_element_type=f32)
        dn = lax.dot_general(gb, qb, (((0,), (0,)), ((), ())), preferred_element_type=f32)
        dn_f[k, at] = dn.reshape(4, n_rows, 256)
        dn_b[k, at] = dn.astype(bf16).reshape(4, n_rows, 256)
        for p in (1, 2, 3):
            to = hop(y, p)
            send(k, RS_Y + 3 * o + p - 1, dn_b.at[k, at, to], rs_y.at[k, at, p], device(y_=to))

    def scatter_y(k):
        for o in (3, 2, 1, 0):
            at = hop(z_lo, 4 - o)
            total = dn_f[k, at, y]
            for p in (1, 2, 3):
                got = rs_y.at[k, at, p]
                remote(k, RS_Y + 3 * o + p - 1, got, got, across).wait_recv()
                total = total + rs_y[k, at, p].astype(f32)
            if o:
                z_b[k, o] = total.astype(bf16)
                send(k, RS_Z + o - 1, z_b.at[k, o], rs_z.at[k, o], device(z_lo_=at))
            else:
                own = total
        return own

    def scatter_z(k, total):
        for o in (1, 2, 3):
            got = rs_z.at[k, o]
            remote(k, RS_Z + o - 1, got, got, across).wait_recv()
            total = total + rs_z[k, o].astype(f32)
        return total

    def own_grad_t(k, total):
        return exact_dot(spread(nidx[:, k * half : (k + 1) * half], 256), total)

    def finish_edges(k):
        d = dq[...]
        dr = back(d, s_v[...])
        total = exact_dot(spread(ridx[k : k + 1, :], 512), dr)
        gr[k, 0] = total[:, :128].reshape(16, 32, 128)
        gr[k, 1] = total[:, 128:].reshape(16, 32, 128)
        send(k, PAIR_A, gr.at[k, 1 - core], pair.at[k], other)

    def finish_s(k):
        ds = back(dq[...], r_v[...])
        g = exact_dot(spread(sidx[k : k + 1, :], 256), ds)
        s_tab[...], s_st[...] = adagrad(s_tab[...], s_st[...], g)

    def rel_pair(k):
        remote(k, PAIR_A, pair.at[k], pair.at[k], other).wait_recv()
        part[k] = gr[k, core] + pair[k]

        def one(o, _):
            p, dev = at_spot(o)
            remote(k, XY_A + o, part.at[k, p], xy.at[k, o], dev).start()
            return 0

        lax.fori_loop(1, 16, one, 0)

    def rel_xy(k):
        total = part[k, spot]
        for o in range(1, 16):
            remote(k, XY_A + o, xy.at[k, o], xy.at[k, o], across).wait_recv()
            total = total + xy[k, o]
        piece[k] = total.reshape(4, 8, 128)
        for o in (1, 2, 3):
            to = hop(z_lo, o)
            send(k, ZL_A + o - 1, piece.at[k, to], zl.at[k, o], device(z_lo_=to))

    def rel_zl(k):
        total = piece[k, z_lo]
        for o in (1, 2, 3):
            remote(k, ZL_A + o - 1, zl.at[k, o], zl.at[k, o], across).wait_recv()
            total = total + zl[k, o]
        zh[k, z_hi] = total
        own = zh.at[k, z_hi]
        for o in (1, 2, 3):
            send(k, ZH + o - 1, own, own, device(z_hi_=hop(z_hi, o)))

    def rel_zh(k):
        for o in (1, 2, 3):
            got = zh.at[k, hop(z_hi, 4 - o)]
            remote(k, ZH + o - 1, got, got, across).wait_recv()
        total = zh[k, 0] + zh[k, 1] + zh[k, 2] + zh[k, 3]
        done[k, core, spot, z_lo] = total
        own = done.at[k, core, spot, z_lo]
        for o in (1, 2, 3):
            send(k, ZL_B + o - 1, own, own, device(z_lo_=hop(z_lo, o)))

    def rel_back(k):
        for o in (1, 2, 3):
            got = done.at[k, core, spot, hop(z_lo, 4 - o)]
            remote(k, ZL_B + o - 1, got, got, across).wait_recv()
        own = done.at[k, core, spot]

        def one(o, _):
            remote(k, XY_B + o, own, own, at_spot(o)[1]).start()
            return 0

        lax.fori_loop(1, 16, one, 0)

    def rel_fill(k):
        def one(o, _):
            got = done.at[k, core, (spot + 16 - o) % 16]
            remote(k, XY_B + o, got, got, across).wait_recv()
            return 0

        lax.fori_loop(1, 16, one, 0)
        send(k, PAIR_B, done.at[k, core], done.at[k, core], other)

    def rel_update(k):
        got = done.at[k, 1 - core]
        remote(k, PAIR_B, got, got, other).wait_recv()
        g = jnp.concatenate([done[k, 0].reshape(512, 128), done[k, 1].reshape(512, 128)], axis=1)
        r_tab[...], r_st[...] = adagrad(r_tab[...], r_st[...], g)

    my_negs(0, t_in[...])
    pl.semaphore_wait(barrier, 22)
    send_negs(0)

    s_tab[...] = s_in[...]
    s_st[...] = columns(ss_in[...])
    t_st[...] = columns(ts_in[...])
    r_tab[...] = jnp.zeros_like(r_tab)
    r_tab[:rels] = r_in[...]
    r_st[...] = jnp.ones_like(r_st)
    r_st[:rels] = columns(rs_in[...])[:rels]
    gather_st(0, t_in[...])
    forward_negs(0)
    gather_r(0)
    g_t = edges(0)
    for o in range(4):
        wait_group(0, o)
        group(0, o)
    finish_edges(0)
    own = scatter_y(0)
    rel_pair(0)
    finish_s(0)
    own = scatter_z(0, own)
    new, state = adagrad(t_in[...], t_st[...], g_t + own_grad_t(0, own))
    t_new[...] = new
    ts_new[...] = state.T[:8]
    send(0, MOVE, t_new, t_got, across)
    send(0, MOVE + 1, ts_new, ts_got, across)
    rel_xy(0)
    rel_zl(0)
    rel_zh(0)
    remote(0, MOVE, t_got, t_got, across).wait_recv()
    my_negs(1, t_got[...])
    send_negs(1)
    rel_back(0)
    remote(0, MOVE + 1, ts_got, ts_got, across).wait_recv()
    t_st[...] = columns(ts_got[:1, :])
    gather_st(1, t_got[...])
    rel_fill(0)
    forward_negs(1)
    rel_update(0)

    gather_r(1)
    g_t = edges(1)
    for o in range(4):
        wait_group(1, o)
        group(1, o)
    finish_edges(1)
    own = scatter_y(1)
    rel_pair(1)
    finish_s(1)
    s_out[...] = s_tab[...]
    ss_out[...] = s_st[...].T[:1]
    own = scatter_z(1, own)
    new, state = adagrad(t_got[...], t_st[...], g_t + own_grad_t(1, own))
    t_out[...] = new
    ts_out[...] = state.T[:1]
    rel_xy(1)
    rel_zl(1)
    rel_zh(1)
    rel_back(1)
    rel_fill(1)
    rel_update(1)
    r_out[...] = r_tab[:rels]
    rs_out[...] = r_st[...].T[:1, :rels]

    for copy in waits:
        copy.wait_send()
    for k in range(2):
        def one(o, _):
            p, dev = at_spot(o)
            remote(k, XY_A + o, part.at[k, p], xy.at[k, o], dev).wait_send()
            own = done.at[k, core, spot]
            remote(k, XY_B + o, own, own, dev).wait_send()
            return 0

        lax.fori_loop(1, 16, one, 0)


def shards(src_table, src_state, dst_table, dst_state, relations, rel_state, src_rows, dst_rows, rel_ids, neg_rows):
    rows, d = src_table.shape
    rels, edges, n = relations.shape[0], src_rows.shape[1], neg_rows.shape[1]
    vm = pltpu.VMEM
    out = pl.pallas_call(
        kernel,
        out_shape=[
            jax.ShapeDtypeStruct((rows, d), f32),
            jax.ShapeDtypeStruct((1, rows), f32),
            jax.ShapeDtypeStruct((rows, d), f32),
            jax.ShapeDtypeStruct((1, rows), f32),
            jax.ShapeDtypeStruct((rels, d), f32),
            jax.ShapeDtypeStruct((1, rels), f32),
        ],
        in_specs=[pl.BlockSpec(memory_space=vm)] * 10,
        out_specs=[pl.BlockSpec(memory_space=vm)] * 6,
        scratch_shapes=[
            vm((2, 4, 4, n, d), bf16),
            vm((2, 4, 4, n, d), f32),
            vm((2, 4, 4, n, d), bf16),
            vm((2, 4, 4, n, d), bf16),
            vm((2, 4, n, d), bf16),
            vm((2, 4, n, d), bf16),
            vm((rows, d), f32),
            vm((8, rows), f32),
            vm((rows, d), f32),
            vm((8, rows), f32),
            vm((2, 2, 16, 32, 128), f32),
            vm((2, 16, 32, 128), f32),
            vm((2, 16, 32, 128), f32),
            vm((2, 16, 32, 128), f32),
            vm((2, 4, 8, 128), f32),
            vm((2, 4, 8, 128), f32),
            vm((2, 8, 128), f32),
            vm((2, 4, 8, 128), f32),
            vm((2, 2, 16, 4, 8, 128), f32),
            vm((rows, d), f32),
            vm((rows, 128), f32),
            vm((rows, 128), f32),
            vm((512, d), f32),
            vm((512, 128), f32),
            vm((edges, d), bf16),
            vm((edges, d), f32),
            vm((edges, d), f32),
            vm((edges, d), f32),
            vm((edges, d), f32),
            pltpu.SemaphoreType.DMA((2, SEMS)),
            pltpu.SemaphoreType.DMA((2, SEMS)),
        ],
        compiler_params=pltpu.CompilerParams(
            collective_id=0, has_side_effects=True, vmem_limit_bytes=48 * 1024 * 1024
        ),
    )(
        src_table, src_state.reshape(1, rows), dst_table, dst_state.reshape(1, rows),
        relations, rel_state.reshape(1, rels), src_rows, dst_rows, rel_ids, neg_rows.reshape(1, 2 * n),
    )
    s, ss, t, ts, r, rs = out
    return s, ss.reshape(rows), t, ts.reshape(rows), r, rs.reshape(rels)


def solution(mesh):
    both = ("dom", "cuts")
    return jax.shard_map(
        shards,
        mesh=mesh,
        in_specs=(P(both, None), P(both), P(both, None), P(both), P(), P()) + (P(None, both),) * 4,
        out_specs=(P(both, None), P(both), P(both, None), P(both), P(), P()),
        check_vma=False,
    )
```

```python
import functools

import jax
import jax.numpy as jnp
from jax import lax
from jax.experimental import pallas as pl
from jax.experimental.pallas import tpu as pltpu
from jax.sharding import PartitionSpec as P

RATE = 0.1
MESH = pl.DeviceIdType.MESH
f32, bf16, i32 = jnp.float32, jnp.bfloat16, jnp.int32

AG_Z, AG_Y, AG_F = 0, 3, 6
RS_Y, RS_Z = 15, 27
IDX, EARLY, LATE, PAIR_A, ZL_B, PAIR_B = 30, 31, 33, 35, 36, 39
XY_A, Z_A, XY_B = 43, 59, 75
SEMS = 139


def split2(x):
    hi = x.astype(bf16)
    return hi, (x - hi.astype(f32)).astype(bf16)


def columns(row):
    return jnp.broadcast_to(row, (128, row.shape[1])).T


def pick(col_idx, width):
    lane = lax.broadcasted_iota(i32, col_idx.shape, 1)
    parts = [jnp.where(col_idx == lane + 128 * j, 1.0, 0.0) for j in range(width // 128)]
    return jnp.concatenate(parts, axis=1).astype(bf16)


def spread(row_idx, width):
    at = lax.broadcasted_iota(i32, (width, row_idx.shape[1]), 0)
    return jnp.where(at == row_idx, 1.0, 0.0).astype(bf16)


def exact_dot(ones, x):
    wide = x.shape[1]
    out = jnp.dot(ones, jnp.concatenate(split2(x), axis=1), preferred_element_type=f32)
    return out[:, :wide] + out[:, wide:]


def back(grad, other):
    h = grad.shape[1] // 2
    gr, gi, orr, oi = grad[:, :h], grad[:, h:], other[:, :h], other[:, h:]
    return jnp.concatenate([gr * orr + gi * oi, gi * orr - gr * oi], axis=1)


def adagrad(w, state, g):
    state = state + jnp.sum(g * g, axis=1, keepdims=True) * (1.0 / g.shape[1])
    scale = RATE / jnp.sqrt(state)
    return w - g * jnp.concatenate([scale] * (g.shape[1] // 128), axis=1), state


def kernel(
    s_hbm, ss_hbm, t_hbm, ts_hbm, r_hbm, rs_hbm, sidx_hbm, didx_hbm, ridx_hbm, nidx_hbm,
    s_tab, ss_out, t_out, ts_out, r_out, rs_out,
    ss_in, t_in, ts_in, r_tab, rs_in, sidx, didx, ridx, nidx,
    negs, dn_f, dn_b, rs_y, z_b, rs_z,
    n_f, n_got, t_soon, ts_soon, t_got, ts_got, late, late_st, late_got, late_st_got,
    gr, pair, part, xy, piece, zs, done,
    s_st, t_st, t_tab, r_st, at_s, at_t, at_r, pick_r, g_r,
    q_v, t_v, r_v, s_v, dq,
    in_sem, ssem, rsem,
):
    dom, cuts = lax.axis_index("dom"), lax.axis_index("cuts")
    x, z_hi, core = dom // 8, (dom // 2) % 4, dom % 2
    z_lo, y = cuts // 4, cuts % 4
    spot, z = x * 4 + y, z_hi * 4 + z_lo
    rels = r_hbm.shape[0]
    n = nidx.shape[1]
    waits = []

    def device(x_=None, z_=None, core_=None, y_=None):
        a = x if x_ is None else x_
        b = z if z_ is None else z_
        c = core if core_ is None else core_
        d = y if y_ is None else y_
        return (a * 8 + (b // 4) * 2 + c, (b % 4) * 4 + d)

    def hop(v, o):
        return (v + o) % 4

    def z_line(o):
        return device(z_=z_hi * 4 + hop(z_lo, o))

    def at_spot(o):
        p = (spot + o) % 16
        return p, device(x_=p // 4, y_=p % 4)

    def at_z(o):
        p = (z + o) % 16
        return p, device(z_=p)

    def remote(k, n, src, dst, dev):
        return pltpu.make_async_remote_copy(
            src_ref=src, dst_ref=dst, send_sem=ssem.at[k, n], recv_sem=rsem.at[k, n],
            device_id=dev, device_id_type=MESH,
        )

    def send(*args):
        copy = remote(*args)
        copy.start()
        waits.append(copy)

    def recv(k, n, ref):
        remote(k, n, ref, ref, other).wait_recv()

    other = device(core_=1 - core)
    across = device(x_=hop(x, 2))

    barrier = pltpu.get_barrier_semaphore()

    def greet(o, _):
        pl.semaphore_signal(barrier, inc=1, device_id=at_z(o)[1], device_id_type=MESH)
        pl.semaphore_signal(barrier, inc=1, device_id=at_spot(o)[1], device_id_type=MESH)
        return 0

    lax.fori_loop(1, 16, greet, 0)
    pl.semaphore_signal(barrier, inc=1, device_id=other, device_id_type=MESH)

    ins = [
        (nidx_hbm, nidx), (t_hbm, t_in), (didx_hbm, didx), (sidx_hbm, sidx), (s_hbm, s_tab),
        (ridx_hbm, ridx), (r_hbm, r_tab.at[pl.ds(0, rels)]), (ts_hbm, ts_in), (ss_hbm, ss_in), (rs_hbm, rs_in),
    ]
    loads = [pltpu.make_async_copy(a, b, in_sem.at[i]) for i, (a, b) in enumerate(ins)]
    for load in loads:
        load.start()

    def neg_row(k):
        return nidx[k : k + 1, :]

    def my_negs(k, table):
        row = jnp.concatenate([neg_row(k), neg_row(k)], axis=1)
        ones = pick(columns(row)[:n], table.shape[0])
        negs[k, z_lo, y] = jnp.dot(ones, table.astype(bf16), preferred_element_type=f32).astype(bf16)

    def send_negs(k):
        own = negs.at[k, z_lo, y]
        for o in (1, 2, 3):
            send(k, AG_Z + o - 1, own, own, z_line(o))
        for o in (1, 2, 3):
            send(k, AG_Y + o - 1, own, own, device(y_=hop(y, o)))

    def forward_negs(k):
        for o in (1, 2, 3):
            block = negs.at[k, hop(z_lo, 4 - o), y]
            recv(k, AG_Z + o - 1, block)
            for p in (1, 2, 3):
                send(k, AG_F + 3 * (o - 1) + p - 1, block, block, device(y_=hop(y, p)))

    def wait_group(k, o):
        first = AG_Y if o == 0 else AG_F + 3 * (o - 1)
        for p in (1, 2, 3):
            recv(k, first + p - 1, negs.at[k, hop(z_lo, 4 - o), hop(y, 4 - p)])

    def place_edges(k):
        at_s[k] = spread(sidx[k : k + 1, :], 256)
        at_t[k] = spread(didx[k : k + 1, :], 256)
        at_r[k] = spread(ridx[k : k + 1, :], rels)
        pick_r[k] = pick(columns(ridx[k : k + 1, :]), 512)

    def gather_s(k):
        s_v[...] = exact_dot(pick(columns(sidx[k : k + 1, :]), 256), s_tab[...])

    def gather_t(k, table):
        t_v[...] = exact_dot(pick(columns(didx[k : k + 1, :]), 256), table)

    def gather_r(k):
        r_v[...] = exact_dot(pick_r[k], r_tab[...])

    def edges(k):
        s, r = s_v[...], r_v[...]
        h = s.shape[1] // 2
        sr, si, rr, ri = s[:, :h], s[:, h:], r[:, :h], r[:, h:]
        q = jnp.concatenate([sr * rr - si * ri, sr * ri + si * rr], axis=1)
        q_v[...] = q.astype(bf16)
        t = t_v[...]
        coef = -jax.nn.sigmoid(-jnp.sum(q * t, axis=1, keepdims=True))
        dq[...] = coef * t
        return exact_dot(at_t[k], coef * q)

    def group(k, o):
        at = hop(z_lo, 4 - o)
        block = negs[k, at].reshape(4 * n, 256)
        qb = q_v[...]
        scores = lax.dot_general(qb, block, (((1,), (1,)), ((), ())), preferred_element_type=f32)
        gb = (jax.nn.sigmoid(scores) * (1.0 / (16 * n))).astype(bf16)
        dn = lax.dot_general(gb, qb, (((0,), (0,)), ((), ())), preferred_element_type=f32)
        dn_f[k, at] = dn.reshape(4, n, 256)
        dn_b[k, at] = dn.astype(bf16).reshape(4, n, 256)
        for p in (1, 2, 3):
            to = hop(y, p)
            send(k, RS_Y + 3 * o + p - 1, dn_b.at[k, at, to], rs_y.at[k, at, p], device(y_=to))
        dq[...] += jnp.dot(gb, block, preferred_element_type=f32)

    def scatter_y(k):
        for o in (1, 2, 3, 0):
            at = hop(z_lo, 4 - o)
            total = dn_f[k, at, y]
            for p in (1, 2, 3):
                recv(k, RS_Y + 3 * o + p - 1, rs_y.at[k, at, p])
                total = total + rs_y[k, at, p].astype(f32)
            if o:
                z_b[k, o] = total.astype(bf16)
                send(k, RS_Z + o - 1, z_b.at[k, o], rs_z.at[k, o], z_line(4 - o))
            else:
                own = total
        return own

    def scatter_z(k, total):
        for o in (1, 2, 3):
            recv(k, RS_Z + o - 1, rs_z.at[k, o])
            total = total + rs_z[k, o].astype(f32)
        return exact_dot(spread(neg_row(k), 256), total)

    def rel_start(k):
        total = exact_dot(at_r[k], back(dq[...], s_v[...]))
        for h in range(2):
            gr[k, h, :rels] = total[:, 128 * h : 128 * h + 128]
            gr[k, h, rels:] = jnp.zeros_like(gr[k, h, rels:])
        send(k, PAIR_A, gr.at[k, 1 - core], pair.at[k], other)

    def finish_s(k):
        g = exact_dot(at_s[k], back(dq[...], r_v[...]))
        s_tab[...], s_st[...] = adagrad(s_tab[...], s_st[...], g)

    def rel_pair(k):
        recv(k, PAIR_A, pair.at[k])
        part[k] = (gr[k, core] + pair[k]).reshape(16, 32, 128)

        def one(o, _):
            p, dev = at_spot(o)
            remote(k, XY_A + o, part.at[k, p], xy.at[k, o], dev).start()
            return 0

        lax.fori_loop(1, 16, one, 0)

    def rel_xy(k):
        total = part[k, spot]
        for o in range(1, 16):
            recv(k, XY_A + o, xy.at[k, o])
            total = total + xy[k, o]
        piece[k] = total.reshape(4, 8, 128)
        zs[k, z] = piece[k, z_lo]

        def one(o, _):
            p, dev = at_z(o)
            remote(k, Z_A + o, piece.at[k, p % 4], zs.at[k, z], dev).start()
            return 0

        lax.fori_loop(1, 16, one, 0)

    def rel_share(k, j, tile):
        def one(o, _):
            remote(k, XY_B + 16 * j + o, tile, tile, at_spot(o)[1]).start()
            return 0

        lax.fori_loop(1, 16, one, 0)

    def rel_z(k):
        for o in range(1, 16):
            recv(k, Z_A + o, zs.at[k, (z + 16 - o) % 16])
        tiles = [zs[k, i] for i in range(16)]
        while len(tiles) > 1:
            tiles = [a + b for a, b in zip(tiles[::2], tiles[1::2])]
        done[k, core, z_lo, spot] = tiles[0]
        own = done.at[k, core, z_lo, spot]
        for o in (1, 2, 3):
            send(k, ZL_B + o - 1, own, own, z_line(o))
        rel_share(k, 0, own)

    def rel_line(k):
        for o in (1, 2, 3):
            got = done.at[k, core, hop(z_lo, 4 - o), spot]
            recv(k, ZL_B + o - 1, got)
            rel_share(k, o, got)

    def rel_back(k):
        for j in range(4):
            at = hop(z_lo, 4 - j)

            def one(o, _):
                recv(k, XY_B + 16 * j + o, done.at[k, core, at, (spot + 16 - o) % 16])
                return 0

            lax.fori_loop(1, 16, one, 0)
            send(k, PAIR_B + j, done.at[k, core, at], done.at[k, core, at], other)

    def rel_update(k):
        for j in range(4):
            recv(k, PAIR_B + j, done.at[k, 1 - core, hop(z_lo, 4 - j)])
        for h in range(2):
            for p in range(16):
                for j in range(4):
                    row = 32 * p + 8 * j
                    if row < rels:
                        g_r[row : row + 8, 128 * h : 128 * h + 128] = done[k, h, j, p]
        return adagrad(r_tab[:rels], r_st[:rels], g_r[...])

    loads[0].wait()
    loads[1].wait()
    my_negs(0, t_in[...])
    n_f[...] = jnp.broadcast_to(jnp.concatenate([neg_row(0), neg_row(0)], axis=1), n_f.shape).astype(f32)
    pl.semaphore_wait(barrier, 31)
    send_negs(0)
    send(0, IDX, n_f, n_got, across)

    for load in loads[2:]:
        load.wait()
    gather_t(0, t_in[...])
    gather_s(0)
    place_edges(0)
    r_tab[rels:] = jnp.zeros_like(r_tab[rels:])
    gather_r(0)
    forward_negs(0)
    t_st[...] = columns(ts_in[...])
    g_t = edges(0)
    soon, state = adagrad(t_in[...], t_st[...], g_t)
    t_soon[...] = soon
    ts_soon[...] = state.T[:8]
    send(0, EARLY, t_soon, t_got, across)
    send(0, EARLY + 1, ts_soon, ts_got, across)
    for o in range(4):
        wait_group(0, o)
        group(0, o)
    rel_start(0)
    s_st[...] = columns(ss_in[...])
    pad = jnp.concatenate([rs_in[...], jnp.ones((1, 512 - rels), f32)], axis=1)
    r_st[...] = columns(pad)
    rel_pair(0)
    own = scatter_y(0)
    finish_s(0)
    rel_xy(0)
    new, state = adagrad(t_in[...], t_st[...], g_t + scatter_z(0, own))
    row = jnp.concatenate([neg_row(0), neg_row(0)], axis=1)
    ones = pick(columns(row)[:n], 256)
    high, rest = split2(new)
    low = (new - high.astype(f32) - rest.astype(f32)).astype(bf16)
    wide = jnp.dot(ones, jnp.concatenate([high, rest, low], axis=1), preferred_element_type=f32)
    late[...] = wide[:, :256] + wide[:, 256:512] + wide[:, 512:]
    late_st[...] = state.T[:8]
    send(0, LATE, late, late_got, across)
    send(0, LATE + 1, late_st, late_st_got, across)
    place_edges(1)
    gather_s(1)
    recv(0, IDX, n_got)
    row = n_got[:1, :].astype(i32)
    col = columns(row)
    lane = lax.broadcasted_iota(i32, col.shape, 1)
    before = lax.broadcasted_iota(i32, col.shape, 0) < lane
    again = jnp.max(jnp.where(before & (col == row), 1.0, 0.0), axis=0, keepdims=True)
    row = row[:, :n]
    hits = jnp.where(lax.broadcasted_iota(i32, (256, n), 0) == row, 1.0, 0.0)
    first = (hits * (1.0 - again[:, :n])).astype(bf16)
    hit = jnp.max(hits, axis=1, keepdims=True) > 0.5
    recv(0, EARLY, t_got)
    recv(0, EARLY + 1, ts_got)
    recv(0, LATE, late_got)
    recv(0, LATE + 1, late_st_got)
    x_late = late_got[...]
    high, rest = split2(x_late)
    low = (x_late - high.astype(f32) - rest.astype(f32)).astype(bf16)
    wide = jnp.dot(first, jnp.concatenate([high, rest, low], axis=1), preferred_element_type=f32)
    t_tab[...] = jnp.where(hit, wide[:, :256] + wide[:, 256:512] + wide[:, 512:], t_got[...])
    my_negs(1, t_tab[...])
    send_negs(1)
    rel_z(0)
    t_st[...] = jnp.where(hit, columns(late_st_got[:1, :]), columns(ts_got[:1, :]))
    gather_t(1, t_tab[...])
    forward_negs(1)
    rel_line(0)
    rel_back(0)
    r_tab[:rels], r_st[:rels] = rel_update(0)

    gather_r(1)
    g_t = edges(1)
    for o in range(4):
        wait_group(1, o)
        group(1, o)
    rel_start(1)
    rel_pair(1)
    own = scatter_y(1)
    finish_s(1)
    ss_out[...] = s_st[...].T[:1]
    rel_xy(1)
    t_out[...], state = adagrad(t_tab[...], t_st[...], g_t + scatter_z(1, own))
    ts_out[...] = state.T[:1]
    rel_z(1)
    rel_line(1)
    rel_back(1)
    r_out[...], state = rel_update(1)
    r_st[:rels] = state
    rs_out[...] = r_st[...].T[:1, :rels]

    for copy in waits:
        copy.wait_send()
    for k in range(2):
        def one(o, _):
            p, dev = at_spot(o)
            remote(k, XY_A + o, part.at[k, p], xy.at[k, o], dev).wait_send()
            remote(k, Z_A + o, piece.at[k, z_lo], zs.at[k, z], at_z(o)[1]).wait_send()
            for j in range(4):
                own = done.at[k, core, z_lo, spot]
                remote(k, XY_B + 16 * j + o, own, own, dev).wait_send()
            return 0

        lax.fori_loop(1, 16, one, 0)


def shards(src_table, src_state, dst_table, dst_state, relations, rel_state, src_rows, dst_rows, rel_ids, neg_rows):
    rows, d = src_table.shape
    rels, edges, n = relations.shape[0], src_rows.shape[1], neg_rows.shape[1]
    vm = pltpu.VMEM
    shapes = [
        jax.ShapeDtypeStruct((rows, d), f32),
        jax.ShapeDtypeStruct((1, rows), f32),
        jax.ShapeDtypeStruct((rows, d), f32),
        jax.ShapeDtypeStruct((1, rows), f32),
        jax.ShapeDtypeStruct((rels, d), f32),
        jax.ShapeDtypeStruct((1, rels), f32),
    ]
    out = pl.pallas_call(
        kernel,
        out_shape=shapes,
        in_specs=[pl.BlockSpec(memory_space=pltpu.HBM)] * 10,
        out_specs=[pl.BlockSpec(memory_space=vm)] * 6,
        scratch_shapes=[
            vm((1, rows), f32),
            vm((rows, d), f32),
            vm((1, rows), f32),
            vm((512, d), f32),
            vm((1, rels), f32),
            vm((2, edges), i32),
            vm((2, edges), i32),
            vm((2, edges), i32),
            vm((2, n), i32),
            vm((2, 4, 4, n, d), bf16),
            vm((2, 4, 4, n, d), f32),
            vm((2, 4, 4, n, d), bf16),
            vm((2, 4, 4, n, d), bf16),
            vm((2, 4, n, d), bf16),
            vm((2, 4, n, d), bf16),
            vm((8, 2 * n), f32),
            vm((8, 2 * n), f32),
            vm((rows, d), f32),
            vm((8, rows), f32),
            vm((rows, d), f32),
            vm((8, rows), f32),
            vm((n, d), f32),
            vm((8, rows), f32),
            vm((n, d), f32),
            vm((8, rows), f32),
            vm((2, 2, 512, 128), f32),
            vm((2, 512, 128), f32),
            vm((2, 16, 32, 128), f32),
            vm((2, 16, 32, 128), f32),
            vm((2, 4, 8, 128), f32),
            vm((2, 16, 8, 128), f32),
            vm((2, 2, 4, 16, 8, 128), f32),
            vm((rows, 128), f32),
            vm((rows, 128), f32),
            vm((rows, d), f32),
            vm((512, 128), f32),
            vm((2, rows, edges), bf16),
            vm((2, rows, edges), bf16),
            vm((2, rels, edges), bf16),
            vm((2, edges, 512), bf16),
            vm((rels, d), f32),
            vm((edges, d), bf16),
            vm((edges, d), f32),
            vm((edges, d), f32),
            vm((edges, d), f32),
            vm((edges, d), f32),
            pltpu.SemaphoreType.DMA((10,)),
            pltpu.SemaphoreType.DMA((2, SEMS)),
            pltpu.SemaphoreType.DMA((2, SEMS)),
        ],
        compiler_params=pltpu.CompilerParams(
            collective_id=0, has_side_effects=True, vmem_limit_bytes=62500000
        ),
    )(
        src_table, src_state.reshape(1, rows), dst_table, dst_state.reshape(1, rows),
        relations, rel_state.reshape(1, rels), src_rows, dst_rows, rel_ids, neg_rows,
    )
    s, ss, t, ts, r, rs = out
    return s, ss.reshape(rows), t, ts.reshape(rows), r, rs.reshape(rels)


def solution(mesh):
    both = ("dom", "cuts")
    return jax.shard_map(
        shards,
        mesh=mesh,
        in_specs=(P(both, None), P(both), P(both, None), P(both), P(), P()) + (P(None, both),) * 4,
        out_specs=(P(both, None), P(both), P(both, None), P(both), P(), P()),
        check_vma=False,
    )
```
